32 devices in a mesh: dp: 2 (over core), blk: 8 (over z, x), head: 2 (over y).
Axes of the slice: x: 2, y: 2, z: 4, core: 2. Of those that a mesh axis runs over, the one named last changes fastest.
Arguments:
- queries: bfloat16 [8192, 5120], P(('dp', 'blk'), 'head'), parts along dimension 0, may hold values from -20 to 20, as said below
- keys: bfloat16 [8192, 5120], P(('dp', 'blk'), 'head'), parts along dimension 0, may hold values from -20 to 20
- values: bfloat16 [8192, 5120], P(('dp', 'blk'), 'head'), parts along dimension 0, may hold values from -6 to 6
- block_list: int32 [64, 16], P(('dp', 'blk')), parts along dimension 0, may hold values from 0 to 31, as said below
- block_count: int32 [64], P(('dp', 'blk')), parts along dimension 0, may hold values from 4 to 16, as said below
- out_weight: bfloat16 [5120, 5120], P('head'), may hold values from -0.25 to 0.25
Outputs:
- projected: bfloat16 [8192, 5120], P(('dp', 'blk', 'head')), parts along dimension 0
The draws below stay inside these ranges and needn't reach their ends.
There are 2 independent parts, one for each index of `dp`. The reference program is written for one: setup_inputs(seed, part) draws one part's arguments, and reference() takes and returns one part's arrays. A program takes and returns all parts, laid end to end along the dimension named above; an argument that names none is the same for every part. Nothing has to cross between parts.
Inputs may be any that keep to these rules, and one draw needn't show every extreme that they name: `block_list`: each row names 16 different key blocks of the same clip; its first entry is the query block itself; only the first block_count entries of a row are used. `block_count`: some query block uses all 16 entries in every draw. `queries`: query entries lie in the stated range.
All inputs are finite; a program needn't handle non-finite values.
Results may differ from the reference program's by a relative error of at most 0.02.
Values may be sent and summed in bfloat16 or wider, within the bound.
A program may use at most 192 MiB of HBM per device.

```python
import math
import jax
import jax.numpy as jnp
from jax import lax

HEADS = 40
HD = 128
BS = 128
KB = 16
D = 5120
SEQ = 4096
NBLK = 32
N_HEAD = 2


def paired_fields(key):
    folded = jax.random.fold_in(key, 17)
    key_query, key_key = jax.random.split(folded, 2)
    query_part = 1.5 * jnp.clip(jax.random.normal(key_query, (SEQ, D), jnp.float32), -4.0, 4.0)
    key_part = 1.5 * jnp.clip(jax.random.normal(key_key, (SEQ, D), jnp.float32), -4.0, 4.0)
    return (query_part, key_part)


def draw_queries(key, part):
    return paired_fields(key)[0].astype(jnp.bfloat16)


def draw_keys(key, part):
    return paired_fields(key)[1].astype(jnp.bfloat16)


def mask_tables(key):
    folded = jax.random.fold_in(key, 23)
    key_order, key_start, key_count = jax.random.split(folded, 3)
    blocks = jnp.arange(NBLK, dtype=jnp.int32)
    distance = jnp.abs(blocks[:, None] - blocks[None, :])
    ranking = jax.random.randint(key_order, (NBLK, NBLK), 0, 65536, dtype=jnp.int32)
    ranking = ranking + jnp.where(distance == 1, 32768, 0) + jnp.where(distance == 0, 1048576, 0)
    ranking = ranking * NBLK + blocks[None, :]
    unused, lists = lax.top_k(ranking, KB)
    busy_start = jax.random.randint(key_start, (), 0, NBLK, dtype=jnp.int32)
    busy_blocks = (blocks - busy_start) % NBLK < max(NBLK // 4, 1)
    others = jax.random.randint(key_count, (NBLK,), max(KB // 4, 1), KB // 2 + 1, dtype=jnp.int32)
    counts = jnp.where(busy_blocks, KB, others)
    return (lists.astype(jnp.int32), counts.astype(jnp.int32))


def draw_block_list(key, part):
    return mask_tables(key)[0]


def draw_block_count(key, part):
    return mask_tables(key)[1]


def steps_of(stream_key, shape, shards, least, largest):
    def one(position, shards_of):
        heights = jax.random.uniform(jax.random.fold_in(jax.random.fold_in(stream_key, 6), position), (shards_of,), jnp.float32, least / len(shards), largest / len(shards))
        return jnp.repeat(jnp.exp(heights), shape[position] // shards_of).reshape((-1,) + (1,) * (len(shape) - position - 1))

    factor_of = one(*shards[0])
    for cut in shards[1:]:
        factor_of = factor_of * one(*cut)
    return factor_of


def gaussian(rng, dims, spread, limit, shards=(), held_as=jnp.bfloat16):
    loudness = steps_of(rng, dims, shards, -0.22, 0.18) if shards else 1.0
    result = jax.random.normal(rng, dims, jnp.float32) * spread * loudness
    return jnp.minimum(jnp.maximum(result, -limit), limit).astype(held_as)


def setup_inputs(seed: int = 0, part: int = 0) -> dict:
    splits = jax.random.split(jax.random.key(seed), 7)
    part_splits = jax.random.split(jax.random.fold_in(splits[6], part), 7)
    queries = draw_queries(jax.random.fold_in(jax.random.fold_in(splits[6], part), 71), part)
    keys = draw_keys(jax.random.fold_in(jax.random.fold_in(splits[6], part), 71), part)
    values = gaussian(part_splits[2], (SEQ, D), 1.0, 6.0, ((0, 8), (1, 2)))
    block_list = draw_block_list(jax.random.fold_in(jax.random.fold_in(splits[6], part), 71), part)
    block_count = draw_block_count(jax.random.fold_in(jax.random.fold_in(splits[6], part), 71), part)
    out_weight = gaussian(splits[5], (D, D), (D // 8) ** -0.5, 0.25, ((0, 2),))
    return dict(queries=queries, keys=keys, values=values, block_list=block_list, block_count=block_count, out_weight=out_weight)


def attend_block(block_index, query_grid, key_grid, value_grid, block_list, block_count):
    chosen = block_list[block_index].astype(jnp.int32)
    key_rows = key_grid[chosen].reshape(KB * BS, HEADS, HD).astype(jnp.float32)
    value_rows = value_grid[chosen].reshape(KB * BS, HEADS, HD).astype(jnp.float32)
    usable = jnp.repeat(jnp.arange(KB, dtype=jnp.int32) < block_count[block_index], BS)
    query_rows = query_grid[block_index].astype(jnp.float32)
    scores = jnp.einsum('qhd,khd->hqk', query_rows, key_rows) * (1.0 / math.sqrt(HD))
    scores = jnp.where(usable[None, None, :], scores, -jnp.inf)
    highest = lax.optimization_barrier(jnp.max(scores, axis=-1, keepdims=True))
    weights = jnp.where(usable[None, None, :], jnp.exp(scores - highest), 0.0)
    totals = lax.optimization_barrier(jnp.sum(weights, axis=-1))
    rounded = lax.optimization_barrier(weights.astype(jnp.bfloat16)).astype(jnp.float32)
    mixed = jnp.einsum('hqk,khd->qhd', rounded, value_rows)
    return (mixed / jnp.transpose(totals)[:, :, None]).astype(jnp.bfloat16).reshape(BS, D)

def reference(queries, keys, values, block_list, block_count, out_weight):
    query_grid = queries.reshape(NBLK, BS, HEADS, HD)
    key_grid = keys.reshape(NBLK, BS, HEADS, HD)
    value_grid = values.reshape(NBLK, BS, HEADS, HD)

    def one_block(block_index):
        return attend_block(block_index, query_grid, key_grid, value_grid, block_list, block_count)
    attended = lax.map(one_block, jnp.arange(NBLK, dtype=jnp.int32)).reshape(SEQ, D)
    group_width = D // N_HEAD
    combined = jnp.zeros((SEQ, D), jnp.float32)
    for group in range(N_HEAD):
        part_in = attended[:, group * group_width:(group + 1) * group_width]
        part_weight = out_weight[group * group_width:(group + 1) * group_width, :]
        partial_sum = jnp.dot(part_in, part_weight, preferred_element_type=jnp.float32)
        rounded_sum = lax.optimization_barrier(partial_sum.astype(jnp.bfloat16)).astype(jnp.float32)
        combined = combined + rounded_sum
    return combined.astype(jnp.bfloat16)
```

```python
import functools
import math

import jax
import jax.numpy as jnp
from jax import lax
from jax.experimental import pallas as pl
from jax.experimental.pallas import tpu as pltpu
from jax.sharding import PartitionSpec as P

HD = 128
BS = 128
KB = 16
GROUP = 4


class Plan:
    def __init__(self, heads, devices):
        self.heads, self.devices = heads, devices
        self.parts = 1
        while heads * self.parts % devices:
            self.parts *= 2
        self.each = heads * self.parts // devices
        self.slots = max(
            (self.each * b + self.each - 1) // self.parts - self.each * b // self.parts + 1
            for b in range(devices)
        )

    def first_head(self, handler):
        first = handler * self.each // self.parts
        if isinstance(first, int):
            return min(first, self.heads - self.slots)
        return jnp.minimum(first, self.heads - self.slots)

    def active(self, home, handler, slot):
        unit = (self.first_head(handler) + slot) * self.parts + home * self.parts // self.devices
        return (unit >= handler * self.each) & (unit < handler * self.each + self.each)

    def pairs(self, hop, slot):
        return [
            (home, home ^ hop)
            for home in range(self.devices)
            if self.active(home, home ^ hop, slot)
        ]


def pack(plan, slot, queries, keys, values):
    rows = queries.shape[0]
    count = plan.devices

    def body(q_ref, k_ref, v_ref, *rest):
        q_outs, kv_outs, sems = rest[:count], rest[count : 2 * count], rest[2 * count]
        me = lax.axis_index("blk")
        copies = []
        for hop in range(count):
            head = plan.first_head(me ^ hop) + slot
            columns = pl.ds(pl.multiple_of(head * HD, HD), HD)
            for n, (src, dst) in enumerate(
                ((k_ref, kv_outs[hop].at[0]), (v_ref, kv_outs[hop].at[1]), (q_ref, q_outs[hop]))
            ):
                copy = pltpu.make_async_copy(src.at[:, columns], dst, sems.at[hop, n])
                copy.start()
                copies.append(copy)
        for copy in copies:
            copy.wait()

    any_spec = pl.BlockSpec(memory_space=pl.ANY)
    outs = pl.pallas_call(
        body,
        out_shape=[jax.ShapeDtypeStruct((rows, HD), queries.dtype)] * count
        + [jax.ShapeDtypeStruct((2, rows, HD), queries.dtype)] * count,
        in_specs=[any_spec] * 3,
        out_specs=[any_spec] * (2 * count),
        scratch_shapes=[pltpu.SemaphoreType.DMA((count, 3))],
        cost_estimate=pl.CostEstimate(
            flops=0, bytes_accessed=12 * count * rows * HD, transcendentals=0
        ),
    )(queries, keys, values)
    return outs[:count], outs[count:]


def attend(plan, lists, counts, query_parts, kv_parts):
    count = plan.devices
    rows = query_parts[0].shape[0]
    blocks = rows // BS
    factor = math.log2(math.e) / math.sqrt(HD)

    def body(list_ref, count_ref, *rest):
        q_in, kv_in = rest[:count], rest[count : 2 * count]
        outs = rest[2 * count : 3 * count]
        q_ref, kv_ref, o_ref, s_ref, sems = rest[3 * count :]
        copies = []
        for hop in range(count):
            copies.append(pltpu.make_async_copy(kv_in[hop], kv_ref.at[hop], sems.at[0, hop]))
            copies.append(pltpu.make_async_copy(q_in[hop], q_ref.at[hop], sems.at[1, hop]))
        for copy in copies:
            copy.start()
        for copy in copies:
            copy.wait()

        def one(i, carry):
            used = count_ref[i]
            hop = i // blocks
            span = pl.ds(pl.multiple_of(lax.rem(i, blocks) * BS, BS), BS)

            @pl.when(used > 0)
            def _():
                query = q_ref[hop, span, :]
                groups = (used + GROUP - 1) // GROUP

                def score(g, highest):
                    for j in range(GROUP):
                        place = g * GROUP + j
                        at = list_ref[i * KB + place]
                        key = kv_ref[
                            at // blocks, 0, pl.ds(pl.multiple_of(lax.rem(at, blocks) * BS, BS), BS), :
                        ]
                        scores = lax.dot_general(
                            query, key, (((1,), (1,)), ((), ())), preferred_element_type=jnp.float32
                        )
                        scores = jnp.where(place < used, scores, -1e30)
                        s_ref[place] = scores
                        highest = jnp.maximum(highest, scores)
                    return highest

                highest = lax.fori_loop(
                    0, groups, score, jnp.full((BS, BS), -1e30, jnp.float32)
                )
                highest = jnp.max(highest, axis=1, keepdims=True)

                def weigh(g, state):
                    total, mixed = state
                    for j in range(GROUP):
                        place = g * GROUP + j
                        at = list_ref[i * KB + place]
                        value = kv_ref[
                            at // blocks, 1, pl.ds(pl.multiple_of(lax.rem(at, blocks) * BS, BS), BS), :
                        ]
                        weights = jnp.exp2((s_ref[place] - highest) * factor)
                        total = total + weights
                        mixed = mixed + jnp.dot(
                            weights.astype(jnp.bfloat16), value, preferred_element_type=jnp.float32
                        )
                    return total, mixed

                zero = jnp.zeros((BS, BS), jnp.float32)
                total, mixed = lax.fori_loop(0, groups, weigh, (zero, zero))
                total = jnp.sum(total, axis=1, keepdims=True)
                o_ref[hop, span, :] = (mixed / total).astype(jnp.bfloat16)

            return carry

        lax.fori_loop(0, count * blocks, one, 0)
        copies = [
            pltpu.make_async_copy(o_ref.at[hop], outs[hop], sems.at[0, hop])
            for hop in range(count)
        ]
        for copy in copies:
            copy.start()
        for copy in copies:
            copy.wait()

    any_spec = pl.BlockSpec(memory_space=pl.ANY)
    smem = pl.BlockSpec(memory_space=pltpu.SMEM)
    return pl.pallas_call(
        body,
        out_shape=[jax.ShapeDtypeStruct((rows, HD), jnp.bfloat16)] * count,
        in_specs=[smem, smem] + [any_spec] * (2 * count),
        out_specs=[any_spec] * count,
        scratch_shapes=[
            pltpu.VMEM((count, rows, HD), jnp.bfloat16),
            pltpu.VMEM((count, 2, rows, HD), jnp.bfloat16),
            pltpu.VMEM((count, rows, HD), jnp.bfloat16),
            pltpu.VMEM((KB, BS, BS), jnp.float32),
            pltpu.SemaphoreType.DMA((2, count)),
        ],
        compiler_params=pltpu.CompilerParams(vmem_limit_bytes=32 * 1024 * 1024),
        cost_estimate=pl.CostEstimate(
            flops=4 * count * rows * BS * HD * KB,
            bytes_accessed=8 * count * rows * HD,
            transcendentals=count * rows * BS * KB,
        ),
    )(lists, counts, *query_parts, *kv_parts)


def unpack(plan, returned):
    rows = returned[0][0].shape[0]
    count = plan.devices

    def body(*refs):
        parts, out_ref, sems = refs[:-2], refs[-2], refs[-1]
        me = lax.axis_index("blk")

        def each(act):
            for slot in range(plan.slots):
                for hop in range(count):
                    handler = me ^ hop
                    head = plan.first_head(handler) + slot
                    columns = pl.ds(pl.multiple_of(head * HD, HD), HD)

                    @pl.when(plan.active(me, handler, slot))
                    def _():
                        act(
                            pltpu.make_async_copy(
                                parts[slot * count + hop], out_ref.at[:, columns], sems.at[slot, hop]
                            )
                        )

        each(lambda copy: copy.start())
        each(lambda copy: copy.wait())

    any_spec = pl.BlockSpec(memory_space=pl.ANY)
    flat = [part for of_slot in returned for part in of_slot]
    return pl.pallas_call(
        body,
        out_shape=jax.ShapeDtypeStruct((rows, plan.heads * HD), jnp.bfloat16),
        in_specs=[any_spec] * len(flat),
        out_specs=any_spec,
        scratch_shapes=[pltpu.SemaphoreType.DMA((plan.slots, count))],
        cost_estimate=pl.CostEstimate(
            flops=0, bytes_accessed=4 * plan.heads * rows * HD, transcendentals=0
        ),
    )(*flat)


def project(attended, out_weight):
    groups = lax.axis_size("head")
    mine = lax.axis_index("head")
    rows = attended.shape[0] // groups
    width = out_weight.shape[1]
    cuts = 4
    piece = width // cuts

    def share(owner, cut):
        return jnp.dot(
            lax.dynamic_slice_in_dim(attended, owner * rows, rows, 0),
            out_weight[:, cut * piece : (cut + 1) * piece],
            preferred_element_type=jnp.float32,
        ).astype(jnp.bfloat16)

    arrived = [
        [
            lax.ppermute(share(mine ^ hop, cut), "head", [(g, g ^ hop) for g in range(groups)])
            for hop in range(1, groups)
        ]
        for cut in range(cuts)
    ]
    done = []
    for cut in range(cuts):
        total = share(mine, cut).astype(jnp.float32)
        for part in arrived[cut]:
            total = total + part.astype(jnp.float32)
        done.append(total.astype(jnp.bfloat16))
    return jnp.concatenate(done, axis=1)


def on_device(queries, keys, values, block_list, block_count, out_weight):
    rows, width = queries.shape
    devices = lax.axis_size("blk")
    me = lax.axis_index("blk")
    plan = Plan(width // HD, devices)
    blocks = rows // BS
    hops = jnp.arange(devices, dtype=jnp.int32)
    homes = me ^ hops
    lists = lax.all_gather(block_list, "blk", axis=0)[homes]
    counts = lax.all_gather(block_count, "blk", axis=0)[homes]
    lists = ((lists // blocks) ^ me) * blocks + lists % blocks
    lists = lists.reshape(-1)

    returned = []
    for slot in range(plan.slots):
        query_parts, kv_parts = pack(plan, slot, queries, keys, values)
        query_parts, kv_parts = list(query_parts), list(kv_parts)
        for hop in range(1, devices):
            kv_parts[hop] = lax.ppermute(
                kv_parts[hop], "blk", [(b, b ^ hop) for b in range(devices)]
            )
            query_parts[hop] = lax.ppermute(query_parts[hop], "blk", plan.pairs(hop, slot))
        handled = jnp.where(plan.active(homes, me, slot)[:, None], counts, 0).reshape(-1)
        results = list(attend(plan, lists, handled, query_parts, kv_parts))
        for hop in range(1, devices):
            results[hop] = lax.ppermute(
                results[hop], "blk", [(handler, home) for home, handler in plan.pairs(hop, slot)]
            )
        returned.append(results)
    return project(unpack(plan, returned), out_weight)


def solution(mesh):
    placed = (
        P(("dp", "blk"), "head"),
        P(("dp", "blk"), "head"),
        P(("dp", "blk"), "head"),
        P(("dp", "blk"), None),
        P(("dp", "blk")),
        P("head", None),
    )
    return jax.shard_map(
        on_device,
        mesh=mesh,
        in_specs=placed,
        out_specs=P(("dp", "blk", "head"), None),
        check_vma=False,
    )
```

```python
import functools
import math

import jax
import jax.numpy as jnp
from jax import lax
from jax.experimental import pallas as pl
from jax.experimental.pallas import tpu as pltpu
from jax.sharding import PartitionSpec as P

HD = 128
BS = 128
KB = 16
GROUP = 8
META = 8
MESH = pl.DeviceIdType.MESH


class Plan:
    def __init__(self, heads, devices):
        self.heads, self.devices = heads, devices
        self.parts = 1
        while heads * self.parts % devices:
            self.parts *= 2
        self.each = heads * self.parts // devices
        firsts = [self.each * b // self.parts for b in range(devices)]
        lasts = [(self.each * b + self.each - 1) // self.parts for b in range(devices)]
        self.slots = max(last - first + 1 for first, last in zip(firsts, lasts))
        self.clipped = max(firsts) > heads - self.slots

    def first_head(self, handler):
        first = handler * self.each // self.parts
        if self.clipped:
            first = jnp.minimum(first, self.heads - self.slots)
        return first

    def handler(self, home, head):
        return (head * self.parts + home * self.parts // self.devices) // self.each

    def active(self, home, handler, slot):
        return self.handler(home, self.first_head(handler) + slot) == handler


def greet(count):
    me = lax.axis_index("blk")
    barrier = pltpu.get_barrier_semaphore()
    for hop in range(1, count):
        pl.semaphore_signal(
            barrier, inc=1, device_id={"blk": (me + hop) % count}, device_id_type=MESH
        )
    pl.semaphore_wait(barrier, count - 1)


def exchange(plan, queries, keys, values, table):
    rows = queries.shape[0]
    count, slots = plan.devices, plan.slots

    def body(q_ref, k_ref, v_ref, t_ref, out, t_out, held, sends, recvs, t_sends, t_recvs, own):
        me = lax.axis_index("blk")

        def big(slot, hop, both):
            part = pl.ds(0, 2) if both else pl.ds(2, 1)
            which = 0 if both else 1
            return pltpu.make_async_remote_copy(
                src_ref=held.at[slot, hop, part],
                dst_ref=out.at[slot, hop, part],
                send_sem=sends.at[slot, hop, which],
                recv_sem=recvs.at[slot, hop, which],
                device_id={"blk": (me + hop) % count},
                device_id_type=MESH,
            )

        def small(hop):
            return pltpu.make_async_remote_copy(
                src_ref=t_ref,
                dst_ref=t_out.at[hop],
                send_sem=t_sends.at[hop],
                recv_sem=t_recvs.at[hop],
                device_id={"blk": (me + hop) % count},
                device_id_type=MESH,
            )

        greet(count)
        own_table = pltpu.make_async_copy(t_ref, t_out.at[0], own.at[slots])
        own_table.start()
        for hop in range(1, count):
            small(hop).start()
        order = sorted(range(1, count), key=lambda hop: -min(hop, count - hop))
        for slot in range(slots):
            for hop in order + [0]:
                handler = (me + hop) % count
                head = plan.first_head(handler) + slot
                columns = pl.ds(pl.multiple_of(head * HD, HD), HD)
                held[slot, hop, 0] = k_ref[:, columns]
                held[slot, hop, 1] = v_ref[:, columns]
                held[slot, hop, 2] = q_ref[:, columns]
                if hop == 0:
                    pltpu.make_async_copy(held.at[slot, 0], out.at[slot, 0], own.at[slot]).start()
                    continue
                big(slot, hop, True).start()

                @pl.when(plan.active(me, handler, slot))
                def _():
                    big(slot, hop, False).start()

        for slot in range(slots):
            for hop in range(1, count):
                big(slot, hop, True).wait()

                @pl.when(plan.active(me, (me + hop) % count, slot))
                def _():
                    big(slot, hop, False).wait_send()

                @pl.when(plan.active((me + count - hop) % count, me, slot))
                def _():
                    big(slot, hop, False).wait_recv()

            pltpu.make_async_copy(held.at[slot, 0], out.at[slot, 0], own.at[slot]).wait()
        for hop in range(1, count):
            small(hop).wait()
        own_table.wait()

    any_spec = pl.BlockSpec(memory_space=pl.ANY)
    vmem = pl.BlockSpec(memory_space=pltpu.VMEM)
    dma = pltpu.SemaphoreType.DMA
    return pl.pallas_call(
        body,
        out_shape=[
            jax.ShapeDtypeStruct((slots, count, 3, rows, HD), queries.dtype),
            jax.ShapeDtypeStruct((count, META, HD), jnp.int32),
        ],
        in_specs=[vmem] * 4,
        out_specs=[any_spec] * 2,
        scratch_shapes=[
            pltpu.VMEM((slots, count, 3, rows, HD), queries.dtype),
            dma((slots, count, 2)),
            dma((slots, count, 2)),
            dma((count,)),
            dma((count,)),
            dma((slots + 1,)),
        ],
        compiler_params=pltpu.CompilerParams(
            collective_id=0, has_side_effects=True, vmem_limit_bytes=48 * 1024 * 1024
        ),
        cost_estimate=pl.CostEstimate(
            flops=0, bytes_accessed=12 * slots * count * rows * HD, transcendentals=0
        ),
    )(queries, keys, values, table)


def attend(plan, lists, counts, packed):
    slots, count, _, rows, _ = packed.shape
    blocks = rows // BS
    factor = math.log2(math.e) / math.sqrt(HD)

    def body(list_ref, count_ref, in_ref, o_ref, s_ref):
        slot = pl.program_id(0)

        def listed(i, g, j, kind):
            at = list_ref[i * KB + g * GROUP + j]
            span = pl.ds(pl.multiple_of(lax.rem(at, blocks) * BS, BS), BS)
            return in_ref[0, at // blocks, kind, span, :]

        def one(i, carry):
            used = count_ref[slot * count * blocks + i]
            hop = i // blocks
            span = pl.ds(pl.multiple_of(lax.rem(i, blocks) * BS, BS), BS)

            @pl.when(used > 0)
            def _():
                query = in_ref[0, hop, 2, span, :]
                groups = (used + GROUP - 1) // GROUP

                def score(g, highest):
                    for j in range(0, GROUP, 2):
                        key = jnp.concatenate([listed(i, g, j, 0), listed(i, g, j + 1, 0)], axis=0)
                        pair = lax.dot_general(
                            query, key, (((1,), (1,)), ((), ())), preferred_element_type=jnp.float32
                        )
                        for n in range(2):
                            place = g * GROUP + j + n
                            scores = pair[:, n * BS : (n + 1) * BS]
                            scores = jnp.where(place < used, scores, -1e30)
                            s_ref[place] = scores
                            highest = jnp.maximum(highest, scores)
                    return highest

                highest = lax.fori_loop(
                    0, groups, score, jnp.full((BS, BS), -1e30, jnp.float32)
                )
                highest = jnp.max(highest, axis=1, keepdims=True)

                def weigh(g, state):
                    total, mixed = state
                    for j in range(0, GROUP, 2):
                        value = jnp.concatenate(
                            [listed(i, g, j, 1), listed(i, g, j + 1, 1)], axis=0
                        )
                        pair = []
                        for n in range(2):
                            weights = jnp.exp2((s_ref[g * GROUP + j + n] - highest) * factor)
                            total = total + weights
                            pair.append(weights.astype(jnp.bfloat16))
                        mixed = mixed + jnp.dot(
                            jnp.concatenate(pair, axis=1), value, preferred_element_type=jnp.float32
                        )
                    return total, mixed

                zero = jnp.zeros((BS, BS), jnp.float32)
                total, mixed = lax.fori_loop(0, groups, weigh, (zero, zero))
                total = jnp.sum(total, axis=1, keepdims=True)
                o_ref[0, hop, span, :] = (mixed / total).astype(jnp.bfloat16)

            return carry

        lax.fori_loop(0, count * blocks, one, 0)

    smem = pl.BlockSpec(memory_space=pltpu.SMEM)
    return pl.pallas_call(
        body,
        grid=(slots,),
        out_shape=jax.ShapeDtypeStruct((slots, count, rows, HD), jnp.bfloat16),
        in_specs=[
            smem,
            smem,
            pl.BlockSpec((1, count, 3, rows, HD), lambda slot: (slot, 0, 0, 0, 0)),
        ],
        out_specs=pl.BlockSpec((1, count, rows, HD), lambda slot: (slot, 0, 0, 0)),
        scratch_shapes=[pltpu.VMEM((KB, BS, BS), jnp.float32)],
        compiler_params=pltpu.CompilerParams(vmem_limit_bytes=48 * 1024 * 1024),
        cost_estimate=pl.CostEstimate(
            flops=4 * slots * count * rows * BS * HD * KB,
            bytes_accessed=8 * slots * count * rows * HD,
            transcendentals=slots * count * rows * BS * KB,
        ),
    )(lists, counts, packed)


def give_back(plan, results):
    slots, count, rows, _ = results.shape
    heads = plan.heads

    def body(in_ref, out_ref, landed, sends, recvs, own):
        me = lax.axis_index("blk")

        def remote(slot, hop, head):
            return pltpu.make_async_remote_copy(
                src_ref=in_ref.at[slot, hop],
                dst_ref=landed.at[head],
                send_sem=sends.at[slot, hop],
                recv_sem=recvs.at[head],
                device_id={"blk": (me + count - hop) % count},
                device_id_type=MESH,
            )

        def local(slot, head):
            return pltpu.make_async_copy(in_ref.at[slot, 0], landed.at[head], own.at[slot])

        greet(count)
        first = plan.first_head(me)
        for slot in range(slots):
            for hop in range(count):

                @pl.when(plan.active((me + count - hop) % count, me, slot))
                def _():
                    if hop:
                        remote(slot, hop, first + slot).start()
                    else:
                        local(slot, first + slot).start()

        for slot in range(slots):
            for hop in range(count):

                @pl.when(plan.active((me + count - hop) % count, me, slot))
                def _():
                    if hop:
                        remote(slot, hop, first + slot).wait_send()
                    else:
                        local(slot, first + slot).wait()

        for head in range(heads):

            @pl.when(plan.handler(me, head) != me)
            def _():
                remote(0, 1, head).wait_recv()

            out_ref[:, head * HD : (head + 1) * HD] = landed[head]

    vmem = pl.BlockSpec(memory_space=pltpu.VMEM)
    dma = pltpu.SemaphoreType.DMA
    return pl.pallas_call(
        body,
        out_shape=jax.ShapeDtypeStruct((rows, heads * HD), jnp.bfloat16),
        in_specs=[vmem],
        out_specs=vmem,
        scratch_shapes=[
            pltpu.VMEM((heads, rows, HD), jnp.bfloat16),
            dma((slots, count)),
            dma((heads,)),
            dma((slots,)),
        ],
        compiler_params=pltpu.CompilerParams(
            collective_id=1, has_side_effects=True, vmem_limit_bytes=48 * 1024 * 1024
        ),
        cost_estimate=pl.CostEstimate(
            flops=0, bytes_accessed=8 * heads * rows * HD, transcendentals=0
        ),
    )(results)


def project(attended, out_weight):
    groups = lax.axis_size("head")
    mine = lax.axis_index("head")
    rows = attended.shape[0] // groups
    width = out_weight.shape[1]
    cuts = 4
    piece = width // cuts

    def share(owner, cut):
        return jnp.dot(
            lax.dynamic_slice_in_dim(attended, owner * rows, rows, 0),
            out_weight[:, cut * piece : (cut + 1) * piece],
            preferred_element_type=jnp.float32,
        ).astype(jnp.bfloat16)

    arrived = [
        [
            lax.ppermute(share(mine ^ hop, cut), "head", [(g, g ^ hop) for g in range(groups)])
            for hop in range(1, groups)
        ]
        for cut in range(cuts)
    ]
    done = []
    for cut in range(cuts):
        total = share(mine, cut).astype(jnp.float32)
        for part in arrived[cut]:
            total = total + part.astype(jnp.float32)
        done.append(total.astype(jnp.bfloat16))
    return jnp.concatenate(done, axis=1)


def on_device(queries, keys, values, block_list, block_count, out_weight):
    rows, width = queries.shape
    devices = lax.axis_size("blk")
    me = lax.axis_index("blk")
    plan = Plan(width // HD, devices)
    blocks = rows // BS
    table = jnp.concatenate([block_list, block_count[:, None]], axis=1)
    table = jnp.pad(table, ((0, META - blocks), (0, HD - KB - 1)))
    packed, tables = exchange(plan, queries, keys, values, table)
    tables = tables[:, :blocks].reshape(devices * blocks, HD)
    lists, counts = tables[:, :KB], tables[:, KB].reshape(devices, blocks)
    lists = (me - lists // blocks) % devices * blocks + lists % blocks
    homes = (me - jnp.arange(devices, dtype=jnp.int32)) % devices
    handled = [
        jnp.where(plan.active(homes, me, slot)[:, None], counts, 0).reshape(-1)
        for slot in range(plan.slots)
    ]
    results = attend(plan, lists.reshape(-1), jnp.concatenate(handled), packed)
    return project(give_back(plan, results), out_weight)


def solution(mesh):
    placed = (
        P(("dp", "blk"), "head"),
        P(("dp", "blk"), "head"),
        P(("dp", "blk"), "head"),
        P(("dp", "blk"), None),
        P(("dp", "blk")),
        P("head", None),
    )
    return jax.shard_map(
        on_device,
        mesh=mesh,
        in_specs=placed,
        out_specs=P(("dp", "blk", "head"), None),
        check_vma=False,
    )
```

```python
import functools
import math

import jax
import jax.numpy as jnp
from jax import lax
from jax.experimental import pallas as pl
from jax.experimental.pallas import tpu as pltpu
from jax.sharding import PartitionSpec as P

HD = 128
BS = 128
KB = 16
META = 8
MESH = pl.DeviceIdType.MESH


class Plan:
    def __init__(self, heads, devices):
        self.heads, self.devices = heads, devices
        self.parts = 1
        while heads * self.parts % devices:
            self.parts *= 2
        self.each = heads * self.parts // devices
        firsts = [self.each * b // self.parts for b in range(devices)]
        lasts = [(self.each * b + self.each - 1) // self.parts for b in range(devices)]
        self.slots = max(last - first + 1 for first, last in zip(firsts, lasts))
        self.clipped = max(firsts) > heads - self.slots

    def head_of(self, handler, phase):
        first = handler * self.each // self.parts
        if self.clipped:
            first = jnp.minimum(first, self.heads - self.slots)
        late = (handler * self.each % self.parts + self.parts - 1) // self.parts
        return first + (phase + late) % self.slots

    def handler(self, home, head):
        return (head * self.parts + home * self.parts // self.devices) // self.each

    def active(self, home, handler, phase):
        return self.handler(home, self.head_of(handler, phase)) == handler


def greet(count):
    me = lax.axis_index("blk")
    barrier = pltpu.get_barrier_semaphore()
    for hop in range(1, count):
        pl.semaphore_signal(
            barrier, inc=1, device_id={"blk": (me + hop) % count}, device_id_type=MESH
        )
    pl.semaphore_wait(barrier, count - 1)


def attention(plan, queries, keys, values, table):
    rows = queries.shape[0]
    blocks = rows // BS
    count, phases, heads = plan.devices, plan.slots, plan.heads
    factor = math.log2(math.e) / math.sqrt(HD)
    side = 2 if blocks % 2 == 0 else 1

    def body(
        q_ref, k_ref, v_ref, t_ref, out_ref,
        held, results, landed, tables, lists, scores_ref,
        sends, recvs, t_sends, t_recvs, back_sends, back_recvs, own, *got,
    ):
        me = lax.axis_index("blk")

        def big(phase, hop, both):
            part = pl.ds(0, 2) if both else pl.ds(2, 1)
            which = 0 if both else 1
            return pltpu.make_async_remote_copy(
                src_ref=held.at[phase, hop, part],
                dst_ref=got[phase].at[hop, part],
                send_sem=sends.at[phase, hop, which],
                recv_sem=recvs.at[phase, hop, which],
                device_id={"blk": (me + hop) % count},
                device_id_type=MESH,
            )

        def small(hop):
            return pltpu.make_async_remote_copy(
                src_ref=t_ref,
                dst_ref=tables.at[hop],
                send_sem=t_sends.at[hop],
                recv_sem=t_recvs.at[hop],
                device_id={"blk": (me + hop) % count},
                device_id_type=MESH,
            )

        def back(phase, hop, head):
            return pltpu.make_async_remote_copy(
                src_ref=results.at[phase, hop],
                dst_ref=landed.at[head],
                send_sem=back_sends.at[phase, hop],
                recv_sem=back_recvs.at[head],
                device_id={"blk": (me + count - hop) % count},
                device_id_type=MESH,
            )

        def stay(phase, head):
            return pltpu.make_async_copy(results.at[phase, 0], landed.at[head], own.at[phase])

        far_first = sorted(range(1, count), key=lambda hop: -min(hop, count - hop))

        def send(phase):
            for hop in far_first + [0]:
                handler = (me + hop) % count
                head = plan.head_of(handler, phase)
                columns = pl.ds(pl.multiple_of(head * HD, HD), HD)
                into = held.at[phase, hop] if hop else got[phase].at[0]
                into[0] = k_ref[:, columns].reshape(blocks, BS, HD)
                into[1] = v_ref[:, columns].reshape(blocks, BS, HD)
                into[2] = q_ref[:, columns].reshape(blocks, BS, HD)
                if hop:
                    big(phase, hop, True).start()

                    @pl.when(plan.active(me, handler, phase))
                    def _():
                        big(phase, hop, False).start()

        def arrive(phase):
            for hop in range(1, count):
                big(phase, hop, True).wait_recv()

                @pl.when(plan.active((me + count - hop) % count, me, phase))
                def _():
                    big(phase, hop, False).wait_recv()

        def attend_block(phase, hop, block, lane):
            query = got[phase][hop, 2, block]
            used = lists[hop, block, KB]
            places = []
            for j in range(KB):
                at = lists[hop, block, j]
                source = lax.rem(me - lax.div(at, blocks) + count, count)
                places.append((source, lax.rem(at, blocks)))

            def listed(j, kind):
                pair = [got[phase][source, kind, block] for source, block in places[j : j + 2]]
                return jnp.concatenate(pair, axis=0)

            highest = None
            for j in range(0, KB, 2):
                pair = lax.dot_general(
                    query, listed(j, 0), (((1,), (1,)), ((), ())), preferred_element_type=jnp.float32
                )
                for n in range(2):
                    scores = pair[:, n * BS : (n + 1) * BS]
                    if j + n >= 4:
                        unused = jnp.minimum(used - (j + n + 1), 0).astype(jnp.float32)
                        scores = scores + unused * 1e30
                    scores_ref[lane, j + n] = scores
                    highest = scores if highest is None else jnp.maximum(highest, scores)
            highest = jnp.max(highest, axis=1, keepdims=True)
            total = jnp.zeros((BS, BS), jnp.float32)
            mixed = jnp.zeros((BS, HD), jnp.float32)
            for j in range(0, KB, 2):
                pair = []
                for n in range(2):
                    weights = jnp.exp2((scores_ref[lane, j + n] - highest) * factor)
                    total = total + weights
                    pair.append(weights.astype(jnp.bfloat16))
                mixed = mixed + jnp.dot(
                    jnp.concatenate(pair, axis=1), listed(j, 1), preferred_element_type=jnp.float32
                )
            total = jnp.sum(total, axis=1, keepdims=True)
            results[phase, hop, pl.ds(pl.multiple_of(block * BS, BS), BS), :] = (
                mixed / total
            ).astype(jnp.bfloat16)

        def attend(phase):
            head = plan.head_of(me, phase)

            def one_home(turn, carry):
                hop = count - 1 - turn

                @pl.when(plan.active((me + count - hop) % count, me, phase))
                def _():
                    def some(i, carry):
                        for lane in range(side):
                            attend_block(phase, hop, i * side + lane, lane)
                        return carry

                    lax.fori_loop(0, blocks // side, some, 0)

                    @pl.when(hop > 0)
                    def _():
                        back(phase, hop, head).start()

                    @pl.when(hop == 0)
                    def _():
                        stay(phase, head).start()

                return carry

            lax.fori_loop(0, count, one_home, 0)

        greet(count)
        for hop in range(1, count):
            small(hop).start()
        tables[0] = t_ref[...]
        for phase in range(min(2, phases)):
            send(phase)
        for hop in range(1, count):
            small(hop).wait()
        to_scalar = pltpu.make_async_copy(tables, lists, own.at[phases])
        to_scalar.start()
        to_scalar.wait()

        for phase in range(phases):
            arrive(phase)
            if phase + 2 < phases:
                send(phase + 2)
            attend(phase)

        for phase in range(phases):
            for hop in range(1, count):
                big(phase, hop, True).wait_send()

                @pl.when(plan.active(me, (me + hop) % count, phase))
                def _():
                    big(phase, hop, False).wait_send()

            for hop in range(count):

                @pl.when(plan.active((me + count - hop) % count, me, phase))
                def _():
                    if hop:
                        back(phase, hop, plan.head_of(me, phase)).wait_send()
                    else:
                        stay(phase, plan.head_of(me, phase)).wait()

        for head in range(heads):

            @pl.when(plan.handler(me, head) != me)
            def _():
                back(0, 1, head).wait_recv()

            out_ref[:, head * HD : (head + 1) * HD] = landed[head]

    vmem = pl.BlockSpec(memory_space=pltpu.VMEM)
    dma = pltpu.SemaphoreType.DMA
    kind = queries.dtype
    return pl.pallas_call(
        body,
        out_shape=jax.ShapeDtypeStruct((rows, heads * HD), kind),
        in_specs=[vmem] * 4,
        out_specs=vmem,
        scratch_shapes=[
            pltpu.VMEM((phases, count, 3, blocks, BS, HD), kind),
            pltpu.VMEM((phases, count, rows, HD), kind),
            pltpu.VMEM((heads, rows, HD), kind),
            pltpu.VMEM((count, META, HD), jnp.int32),
            pltpu.SMEM((count, META, HD), jnp.int32),
            pltpu.VMEM((side, KB, BS, BS), jnp.float32),
            dma((phases, count, 2)),
            dma((phases, count, 2)),
            dma((count,)),
            dma((count,)),
            dma((phases, count)),
            dma((heads,)),
            dma((phases + 1,)),
        ]
        + [pltpu.VMEM((count, 3, blocks, BS, HD), kind)] * phases,
        compiler_params=pltpu.CompilerParams(
            collective_id=0, has_side_effects=True, vmem_limit_bytes=56 * 1024 * 1024
        ),
        cost_estimate=pl.CostEstimate(
            flops=4 * heads * rows * BS * HD * KB,
            bytes_accessed=8 * heads * rows * HD,
            transcendentals=heads * rows * BS * KB,
        ),
    )(queries, keys, values, table)


def project(attended, out_weight):
    groups = lax.axis_size("head")
    mine = lax.axis_index("head")
    rows = attended.shape[0] // groups
    width = out_weight.shape[1]
    cuts = 4
    piece = width // cuts

    def share(owner, cut):
        return jnp.dot(
            lax.dynamic_slice_in_dim(attended, owner * rows, rows, 0),
            out_weight[:, cut * piece : (cut + 1) * piece],
            preferred_element_type=jnp.float32,
        ).astype(jnp.bfloat16)

    arrived = [
        [
            lax.ppermute(share(mine ^ hop, cut), "head", [(g, g ^ hop) for g in range(groups)])
            for hop in range(1, groups)
        ]
        for cut in range(cuts)
    ]
    done = []
    for cut in range(cuts):
        total = share(mine, cut).astype(jnp.float32)
        for part in arrived[cut]:
            total = total + part.astype(jnp.float32)
        done.append(total.astype(jnp.bfloat16))
    return jnp.concatenate(done, axis=1)


def on_device(queries, keys, values, block_list, block_count, out_weight):
    rows, width = queries.shape
    devices = lax.axis_size("blk")
    plan = Plan(width // HD, devices)
    blocks = rows // BS
    table = jnp.concatenate([block_list, block_count[:, None]], axis=1)
    table = jnp.pad(table, ((0, META - blocks), (0, HD - KB - 1)))
    return project(attention(plan, queries, keys, values, table), out_weight)


def solution(mesh):
    placed = (
        P(("dp", "blk"), "head"),
        P(("dp", "blk"), "head"),
        P(("dp", "blk"), "head"),
        P(("dp", "blk"), None),
        P(("dp", "blk")),
        P("head", None),
    )
    return jax.shard_map(
        on_device,
        mesh=mesh,
        in_specs=placed,
        out_specs=P(("dp", "blk", "head"), None),
        check_vma=False,
    )
```

```python
import functools
import math

import jax
import jax.numpy as jnp
from jax import lax
from jax.experimental import pallas as pl
from jax.experimental.pallas import tpu as pltpu
from jax.sharding import PartitionSpec as P

HD = 128
BS = 128
KB = 16
META = 8
CHUNKS = 5
FETCHED = 3
MESH = pl.DeviceIdType.MESH


class Plan:
    def __init__(self, heads, devices):
        self.heads, self.devices = heads, devices
        self.parts = 1
        while heads * self.parts % devices:
            self.parts *= 2
        self.each = heads * self.parts // devices
        firsts = [self.each * b // self.parts for b in range(devices)]
        lasts = [(self.each * b + self.each - 1) // self.parts for b in range(devices)]
        self.slots = max(last - first + 1 for first, last in zip(firsts, lasts))
        self.clipped = max(firsts) > heads - self.slots

    def head_of(self, handler, phase):
        first = handler * self.each // self.parts
        if self.clipped:
            first = jnp.minimum(first, self.heads - self.slots)
        late = (handler * self.each % self.parts + self.parts - 1) // self.parts
        return first + (phase + late) % self.slots

    def handler(self, home, head):
        return (head * self.parts + home * self.parts // self.devices) // self.each

    def active(self, home, handler, phase):
        return self.handler(home, self.head_of(handler, phase)) == handler


def greet(count, groups):
    me, group, core = (lax.axis_index(name) for name in ("blk", "head", "dp"))
    barrier = pltpu.get_barrier_semaphore()
    for hop in range(count):
        for over in range(groups):
            if hop or over:
                pl.semaphore_signal(
                    barrier,
                    inc=1,
                    device_id={"blk": (me + hop) % count, "head": (group + over) % groups},
                    device_id_type=MESH,
                )
    pl.semaphore_signal(barrier, inc=1, device_id={"dp": 1 - core}, device_id_type=MESH)
    pl.semaphore_wait(barrier, count * groups)


def attention(plan, queries, keys, values, table, out_weight):
    rows = queries.shape[0]
    blocks = rows // BS
    count, phases, heads = plan.devices, plan.slots, plan.heads
    groups = lax.axis_size("head")
    share = rows // groups
    chunk_rows = out_weight.shape[0] // (2 * CHUNKS)
    factor = math.log2(math.e) / math.sqrt(HD)
    side = 2 if blocks % 2 == 0 else 1

    def body(
        q_ref, k_ref, v_ref, t_ref, w_ref, out_ref, w_out,
        held, results, landed, tables, lists, scores_ref,
        sends, recvs, t_sends, t_recvs, back_sends, back_recvs, own,
        y_sends, y_recvs, x_sends, x_recvs, core_sends, core_recvs, *got,
    ):
        me, group, core = (lax.axis_index(name) for name in ("blk", "head", "dp"))
        odd = me % 2

        def big(phase, hop, both):
            part = pl.ds(0, 2) if both else pl.ds(2, 1)
            which = 0 if both else 1
            return pltpu.make_async_remote_copy(
                src_ref=held.at[phase, hop, part],
                dst_ref=got[phase].at[hop, part],
                send_sem=sends.at[phase, hop, which],
                recv_sem=recvs.at[phase, hop, which],
                device_id={"blk": (me + hop) % count},
                device_id_type=MESH,
            )

        def small(hop):
            return pltpu.make_async_remote_copy(
                src_ref=t_ref,
                dst_ref=tables.at[hop],
                send_sem=t_sends.at[hop],
                recv_sem=t_recvs.at[hop],
                device_id={"blk": (me + hop) % count},
                device_id_type=MESH,
            )

        def back(phase, hop, over, head):
            owner = (group + over) % groups
            return pltpu.make_async_remote_copy(
                src_ref=results.at[phase, hop, owner],
                dst_ref=landed.at[over, head],
                send_sem=back_sends.at[phase, hop, over],
                recv_sem=back_recvs.at[over, head],
                device_id={"blk": (me + count - hop) % count, "head": owner},
                device_id_type=MESH,
            )

        def stay(phase, head):
            return pltpu.make_async_copy(
                results.at[phase, 0, group], landed.at[0, head], own.at[phase]
            )

        def chunk(i, side_x):
            place = core * CHUNKS + i + side_x * (CHUNKS - 1 - 2 * i)
            return pl.ds(pl.multiple_of(place * chunk_rows, chunk_rows), chunk_rows)

        def over_y(over, i):
            return pltpu.make_async_remote_copy(
                src_ref=w_ref.at[chunk(i, odd)],
                dst_ref=w_out.at[over - 1, chunk(i, odd)],
                send_sem=y_sends.at[over - 1, i],
                recv_sem=y_recvs.at[over - 1, i],
                device_id={"head": (group + over) % groups},
                device_id_type=MESH,
            )

        def over_x(over, i):
            return pltpu.make_async_remote_copy(
                src_ref=w_out.at[over - 1, chunk(i, odd)],
                dst_ref=w_out.at[over - 1, chunk(i, odd)],
                send_sem=x_sends.at[over - 1, i],
                recv_sem=x_recvs.at[over - 1, i],
                device_id={"blk": me + 1 - 2 * odd},
                device_id_type=MESH,
            )

        def over_core(over, i):
            return pltpu.make_async_remote_copy(
                src_ref=w_out.at[over - 1, chunk(i, odd)],
                dst_ref=w_out.at[over - 1, chunk(i, odd)],
                send_sem=core_sends.at[over - 1, i],
                recv_sem=core_recvs.at[over - 1, i],
                device_id={"dp": 1 - core},
                device_id_type=MESH,
            )

        def pass_on(i):
            for over in range(1, groups):
                if i < FETCHED:
                    over_y(over, i).wait_recv()
                    if i < CHUNKS - FETCHED:
                        over_x(over, i).start()
                else:
                    over_x(over, CHUNKS - 1 - i).wait_recv()
                over_core(over, i).start()

        far_first = sorted(range(1, count), key=lambda hop: -min(hop, count - hop))

        def send(phase):
            for hop in far_first + [0]:
                handler = (me + hop) % count
                head = plan.head_of(handler, phase)
                columns = pl.ds(pl.multiple_of(head * HD, HD), HD)
                into = held.at[phase, hop] if hop else got[phase].at[0]
                into[0] = k_ref[:, columns].reshape(blocks, BS, HD)
                into[1] = v_ref[:, columns].reshape(blocks, BS, HD)
                into[2] = q_ref[:, columns].reshape(blocks, BS, HD)
                if hop:
                    big(phase, hop, True).start()

                    @pl.when(plan.active(me, handler, phase))
                    def _():
                        big(phase, hop, False).start()

        def arrive(phase):
            for hop in range(1, count):
                big(phase, hop, True).wait_recv()

                @pl.when(plan.active((me + count - hop) % count, me, phase))
                def _():
                    big(phase, hop, False).wait_recv()

        def attend_block(phase, hop, block, lane):
            query = got[phase][hop, 2, block]
            used = lists[hop, block, KB]
            places = []
            for j in range(KB):
                at = lists[hop, block, j]
                source = lax.rem(me - lax.div(at, blocks) + count, count)
                places.append((source, lax.rem(at, blocks)))

            def listed(j, kind):
                pair = [got[phase][source, kind, block] for source, block in places[j : j + 2]]
                return jnp.concatenate(pair, axis=0)

            highest = None
            for j in range(0, KB, 2):
                pair = lax.dot_general(
                    query, listed(j, 0), (((1,), (1,)), ((), ())), preferred_element_type=jnp.float32
                )
                for n in range(2):
                    scores = pair[:, n * BS : (n + 1) * BS]
                    if j + n >= 4:
                        unused = jnp.minimum(used - (j + n + 1), 0).astype(jnp.float32)
                        scores = scores + unused * 1e30
                    scores_ref[lane, j + n] = scores
                    highest = scores if highest is None else jnp.maximum(highest, scores)
            highest = jnp.max(highest, axis=1, keepdims=True)
            total = jnp.zeros((BS, BS), jnp.float32)
            mixed = jnp.zeros((BS, HD), jnp.float32)
            for j in range(0, KB, 2):
                pair = []
                for n in range(2):
                    weights = jnp.exp2((scores_ref[lane, j + n] - highest) * factor)
                    total = total + weights
                    pair.append(weights.astype(jnp.bfloat16))
                mixed = mixed + jnp.dot(
                    jnp.concatenate(pair, axis=1), listed(j, 1), preferred_element_type=jnp.float32
                )
            total = jnp.sum(total, axis=1, keepdims=True)
            mixed = (mixed / total).astype(jnp.bfloat16)
            if share >= BS:
                each = share // BS
                span = pl.ds(pl.multiple_of(block % each * BS, BS), BS)
                results[phase, hop, block // each, span, :] = mixed
            else:
                each = BS // share
                results[phase, hop, pl.ds(block * each, each)] = mixed.reshape(each, share, HD)

        def attend(phase):
            head = plan.head_of(me, phase)

            def one_home(turn, carry):
                hop = count - 1 - turn

                @pl.when(plan.active((me + count - hop) % count, me, phase))
                def _():
                    def some(i, carry):
                        for lane in range(side):
                            attend_block(phase, hop, i * side + lane, lane)
                        return carry

                    lax.fori_loop(0, blocks // side, some, 0)

                    for over in range(1, groups):
                        back(phase, hop, over, head).start()

                    @pl.when(hop > 0)
                    def _():
                        back(phase, hop, 0, head).start()

                    @pl.when(hop == 0)
                    def _():
                        stay(phase, head).start()

                return carry

            lax.fori_loop(0, count, one_home, 0)

        greet(count, groups)
        for hop in range(1, count):
            small(hop).start()
        tables[0] = t_ref[...]
        for phase in range(min(2, phases)):
            send(phase)
        for i in range(FETCHED):
            for over in range(1, groups):
                over_y(over, i).start()
        for hop in range(1, count):
            small(hop).wait()
        to_scalar = pltpu.make_async_copy(tables, lists, own.at[phases])
        to_scalar.start()
        to_scalar.wait()

        for phase in range(phases):
            arrive(phase)
            if phase + 2 < phases:
                send(phase + 2)
            if phase:
                for i in range(FETCHED * (phase - 1) // (phases - 1), FETCHED * phase // (phases - 1)):
                    pass_on(i)
            attend(phase)

        for i in range(FETCHED, CHUNKS):
            pass_on(i)
        for phase in range(phases):
            for hop in range(1, count):
                big(phase, hop, True).wait_send()

                @pl.when(plan.active(me, (me + hop) % count, phase))
                def _():
                    big(phase, hop, False).wait_send()

            for hop in range(count):

                @pl.when(plan.active((me + count - hop) % count, me, phase))
                def _():
                    for over in range(groups):
                        if hop or over:
                            back(phase, hop, over, plan.head_of(me, phase)).wait_send()
                        else:
                            stay(phase, plan.head_of(me, phase)).wait()

        for head in range(heads):
            for over in range(groups):
                if over:
                    back(0, 1, over, head).wait_recv()
                else:

                    @pl.when(plan.handler(me, head) != me)
                    def _():
                        back(0, 1, 0, head).wait_recv()

                out_ref[over, :, head * HD : (head + 1) * HD] = landed[over, head]

        for over in range(1, groups):
            for i in range(CHUNKS):
                if i < FETCHED:
                    over_y(over, i).wait_send()
                if i < CHUNKS - FETCHED:
                    over_x(over, i).wait_send()
                over_core(over, i).wait()

    vmem = pl.BlockSpec(memory_space=pltpu.VMEM)
    any_spec = pl.BlockSpec(memory_space=pl.ANY)
    dma = pltpu.SemaphoreType.DMA
    kind = queries.dtype
    return pl.pallas_call(
        body,
        out_shape=[
            jax.ShapeDtypeStruct((groups, share, heads * HD), kind),
            jax.ShapeDtypeStruct((groups - 1, *out_weight.shape), kind),
        ],
        in_specs=[vmem] * 4 + [any_spec],
        out_specs=[vmem, any_spec],
        scratch_shapes=[
            pltpu.VMEM((phases, count, 3, blocks, BS, HD), kind),
            pltpu.VMEM((phases, count, groups, share, HD), kind),
            pltpu.VMEM((groups, heads, share, HD), kind),
            pltpu.VMEM((count, META, HD), jnp.int32),
            pltpu.SMEM((count, META, HD), jnp.int32),
            pltpu.VMEM((side, KB, BS, BS), jnp.float32),
            dma((phases, count, 2)),
            dma((phases, count, 2)),
            dma((count,)),
            dma((count,)),
            dma((phases, count, groups)),
            dma((groups, heads)),
            dma((phases + 1,)),
            dma((groups - 1, FETCHED)),
            dma((groups - 1, FETCHED)),
            dma((groups - 1, CHUNKS - FETCHED)),
            dma((groups - 1, CHUNKS - FETCHED)),
            dma((groups - 1, CHUNKS)),
            dma((groups - 1, CHUNKS)),
        ]
        + [pltpu.VMEM((count, 3, blocks, BS, HD), kind)] * phases,
        compiler_params=pltpu.CompilerParams(
            collective_id=0, has_side_effects=True, vmem_limit_bytes=56 * 1024 * 1024
        ),
        cost_estimate=pl.CostEstimate(
            flops=4 * heads * rows * BS * HD * KB,
            bytes_accessed=8 * heads * rows * HD,
            transcendentals=heads * rows * BS * KB,
        ),
    )(queries, keys, values, table, out_weight)


def project(attended, out_weight, others):
    total = 0.0
    for over in range(attended.shape[0]):
        part = jnp.dot(
            attended[over],
            others[over - 1] if over else out_weight,
            preferred_element_type=jnp.float32,
        )
        total = total + part.astype(jnp.bfloat16).astype(jnp.float32)
    return total.astype(jnp.bfloat16)


def on_device(queries, keys, values, block_list, block_count, out_weight):
    rows, width = queries.shape
    devices = lax.axis_size("blk")
    plan = Plan(width // HD, devices)
    blocks = rows // BS
    table = jnp.concatenate([block_list, block_count[:, None]], axis=1)
    table = jnp.pad(table, ((0, META - blocks), (0, HD - KB - 1)))
    attended, others = attention(plan, queries, keys, values, table, out_weight)
    return project(attended, out_weight, others)


def solution(mesh):
    placed = (
        P(("dp", "blk"), "head"),
        P(("dp", "blk"), "head"),
        P(("dp", "blk"), "head"),
        P(("dp", "blk"), None),
        P(("dp", "blk")),
        P("head", None),
    )
    return jax.shard_map(
        on_device,
        mesh=mesh,
        in_specs=placed,
        out_specs=P(("dp", "blk", "head"), None),
        check_vma=False,
    )
```

```python
import functools
import math

import jax
import jax.numpy as jnp
from jax import lax
from jax.experimental import pallas as pl
from jax.experimental.pallas import tpu as pltpu
from jax.sharding import PartitionSpec as P

HD = 128
BS = 128
KB = 16
META = 8
MESH = pl.DeviceIdType.MESH


class Plan:
    def __init__(self, heads, devices):
        self.heads, self.devices = heads, devices
        self.parts = 1
        while heads * self.parts % devices:
            self.parts *= 2
        self.each = heads * self.parts // devices
        firsts = [self.each * b // self.parts for b in range(devices)]
        lasts = [(self.each * b + self.each - 1) // self.parts for b in range(devices)]
        self.slots = max(last - first + 1 for first, last in zip(firsts, lasts))
        self.clipped = max(firsts) > heads - self.slots

    def head_of(self, handler, phase):
        first = handler * self.each // self.parts
        if self.clipped:
            first = jnp.minimum(first, self.heads - self.slots)
        late = (handler * self.each % self.parts + self.parts - 1) // self.parts
        return first + (phase + late) % self.slots

    def handler(self, home, head):
        return (head * self.parts + home * self.parts // self.devices) // self.each

    def active(self, home, handler, phase):
        return self.handler(home, self.head_of(handler, phase)) == handler


def greet(count):
    me = lax.axis_index("blk")
    barrier = pltpu.get_barrier_semaphore()
    for hop in range(1, count):
        pl.semaphore_signal(
            barrier, inc=1, device_id={"blk": (me + hop) % count}, device_id_type=MESH
        )
    pl.semaphore_wait(barrier, count - 1)


def attention(plan, queries, keys, values, table):
    rows = queries.shape[0]
    blocks = rows // BS
    count, phases, heads = plan.devices, plan.slots, plan.heads
    factor = math.log2(math.e) / math.sqrt(HD)
    side = 2 if blocks % 2 == 0 else 1

    def body(
        q_ref, k_ref, v_ref, t_ref, out_ref,
        held, results, landed, tables, lists, scores_ref,
        sends, recvs, t_sends, t_recvs, back_sends, back_recvs, own, *got,
    ):
        me = lax.axis_index("blk")

        def big(phase, hop, both):
            part = pl.ds(0, 2) if both else pl.ds(2, 1)
            which = 0 if both else 1
            return pltpu.make_async_remote_copy(
                src_ref=held.at[phase, hop, part],
                dst_ref=got[phase].at[hop, part],
                send_sem=sends.at[phase, hop, which],
                recv_sem=recvs.at[phase, hop, which],
                device_id={"blk": (me + hop) % count},
                device_id_type=MESH,
            )

        def small(hop):
            return pltpu.make_async_remote_copy(
                src_ref=t_ref,
                dst_ref=tables.at[hop],
                send_sem=t_sends.at[hop],
                recv_sem=t_recvs.at[hop],
                device_id={"blk": (me + hop) % count},
                device_id_type=MESH,
            )

        def back(phase, hop, head):
            return pltpu.make_async_remote_copy(
                src_ref=results.at[phase, hop],
                dst_ref=landed.at[head],
                send_sem=back_sends.at[phase, hop],
                recv_sem=back_recvs.at[head],
                device_id={"blk": (me + count - hop) % count},
                device_id_type=MESH,
            )

        def stay(phase, head):
            return pltpu.make_async_copy(results.at[phase, 0], landed.at[head], own.at[phase])

        far_first = sorted(range(1, count), key=lambda hop: -min(hop, count - hop))

        def send(phase):
            for hop in far_first + [0]:
                handler = (me + hop) % count
                head = plan.head_of(handler, phase)
                columns = pl.ds(pl.multiple_of(head * HD, HD), HD)
                into = held.at[phase, hop] if hop else got[phase].at[0]
                into[0] = k_ref[:, columns].reshape(blocks, BS, HD)
                into[1] = v_ref[:, columns].reshape(blocks, BS, HD)
                into[2] = q_ref[:, columns].reshape(blocks, BS, HD)
                if hop:
                    big(phase, hop, True).start()

                    @pl.when(plan.active(me, handler, phase))
                    def _():
                        big(phase, hop, False).start()

        def arrive(phase):
            for hop in range(1, count):
                big(phase, hop, True).wait_recv()

                @pl.when(plan.active((me + count - hop) % count, me, phase))
                def _():
                    big(phase, hop, False).wait_recv()

        def attend_block(phase, hop, block, lane):
            query = got[phase][hop, 2, block]
            used = lists[hop, block, KB]
            places = []
            for j in range(KB):
                at = lists[hop, block, j]
                source = lax.rem(me - lax.div(at, blocks) + count, count)
                places.append((source, lax.rem(at, blocks)))

            def listed(j, kind):
                pair = [got[phase][source, kind, block] for source, block in places[j : j + 2]]
                return jnp.concatenate(pair, axis=0)

            highest = None
            for j in range(0, KB, 2):
                pair = lax.dot_general(
                    query, listed(j, 0), (((1,), (1,)), ((), ())), preferred_element_type=jnp.float32
                )
                for n in range(2):
                    scores = pair[:, n * BS : (n + 1) * BS]
                    if j + n >= 4:
                        unused = jnp.minimum(used - (j + n + 1), 0).astype(jnp.float32)
                        scores = scores + unused * 1e30
                    scores_ref[lane, j + n] = scores
                    highest = scores if highest is None else jnp.maximum(highest, scores)
            highest = jnp.max(highest, axis=1, keepdims=True)
            total = jnp.zeros((BS, BS), jnp.float32)
            mixed = jnp.zeros((BS, HD), jnp.float32)
            for j in range(0, KB, 2):
                pair = []
                for n in range(2):
                    weights = jnp.exp2((scores_ref[lane, j + n] - highest) * factor)
                    total = total + weights
                    pair.append(weights.astype(jnp.bfloat16))
                mixed = mixed + jnp.dot(
                    jnp.concatenate(pair, axis=1), listed(j, 1), preferred_element_type=jnp.float32
                )
            total = jnp.sum(total, axis=1, keepdims=True)
            results[phase, hop, pl.ds(pl.multiple_of(block * BS, BS), BS), :] = (
                mixed / total
            ).astype(jnp.bfloat16)

        def attend(phase):
            head = plan.head_of(me, phase)

            def one_home(turn, carry):
                hop = count - 1 - turn

                @pl.when(plan.active((me + count - hop) % count, me, phase))
                def _():
                    def some(i, carry):
                        for lane in range(side):
                            attend_block(phase, hop, i * side + lane, lane)
                        return carry

                    lax.fori_loop(0, blocks // side, some, 0)

                    @pl.when(hop > 0)
                    def _():
                        back(phase, hop, head).start()

                    @pl.when(hop == 0)
                    def _():
                        stay(phase, head).start()

                return carry

            lax.fori_loop(0, count, one_home, 0)

        greet(count)
        for hop in range(1, count):
            small(hop).start()
        tables[0] = t_ref[...]
        for phase in range(min(2, phases)):
            send(phase)
        for hop in range(1, count):
            small(hop).wait()
        to_scalar = pltpu.make_async_copy(tables, lists, own.at[phases])
        to_scalar.start()
        to_scalar.wait()

        for phase in range(phases):
            arrive(phase)
            if phase + 2 < phases:
                send(phase + 2)
            attend(phase)

        for phase in range(phases):
            for hop in range(1, count):
                big(phase, hop, True).wait_send()

                @pl.when(plan.active(me, (me + hop) % count, phase))
                def _():
                    big(phase, hop, False).wait_send()

            for hop in range(count):

                @pl.when(plan.active((me + count - hop) % count, me, phase))
                def _():
                    if hop:
                        back(phase, hop, plan.head_of(me, phase)).wait_send()
                    else:
                        stay(phase, plan.head_of(me, phase)).wait()

        for head in range(heads):

            @pl.when(plan.handler(me, head) != me)
            def _():
                back(0, 1, head).wait_recv()

            out_ref[:, head * HD : (head + 1) * HD] = landed[head]

    vmem = pl.BlockSpec(memory_space=pltpu.VMEM)
    dma = pltpu.SemaphoreType.DMA
    kind = queries.dtype
    return pl.pallas_call(
        body,
        out_shape=jax.ShapeDtypeStruct((rows, heads * HD), kind),
        in_specs=[vmem] * 4,
        out_specs=vmem,
        scratch_shapes=[
            pltpu.VMEM((phases, count, 3, blocks, BS, HD), kind),
            pltpu.VMEM((phases, count, rows, HD), kind),
            pltpu.VMEM((heads, rows, HD), kind),
            pltpu.VMEM((count, META, HD), jnp.int32),
            pltpu.SMEM((count, META, HD), jnp.int32),
            pltpu.VMEM((side, KB, BS, BS), jnp.float32),
            dma((phases, count, 2)),
            dma((phases, count, 2)),
            dma((count,)),
            dma((count,)),
            dma((phases, count)),
            dma((heads,)),
            dma((phases + 1,)),
        ]
        + [pltpu.VMEM((count, 3, blocks, BS, HD), kind)] * phases,
        compiler_params=pltpu.CompilerParams(
            collective_id=0, has_side_effects=True, vmem_limit_bytes=56 * 1024 * 1024
        ),
        cost_estimate=pl.CostEstimate(
            flops=4 * heads * rows * BS * HD * KB,
            bytes_accessed=8 * heads * rows * HD,
            transcendentals=heads * rows * BS * KB,
        ),
    )(queries, keys, values, table)


def project(attended, out_weight):
    groups = lax.axis_size("head")
    mine = lax.axis_index("head")
    rows = attended.shape[0] // groups
    width = out_weight.shape[1]
    cuts = 8
    piece = width // cuts

    def share(owner, cut):
        return jnp.dot(
            lax.dynamic_slice_in_dim(attended, owner * rows, rows, 0),
            out_weight[:, cut * piece : (cut + 1) * piece],
            preferred_element_type=jnp.float32,
        ).astype(jnp.bfloat16)

    arrived = [
        [
            lax.ppermute(share(mine ^ hop, cut), "head", [(g, g ^ hop) for g in range(groups)])
            for hop in range(1, groups)
        ]
        for cut in range(cuts)
    ]
    done = []
    for cut in range(cuts):
        total = share(mine, cut).astype(jnp.float32)
        for part in arrived[cut]:
            total = total + part.astype(jnp.float32)
        done.append(total.astype(jnp.bfloat16))
    return jnp.concatenate(done, axis=1)


def on_device(queries, keys, values, block_list, block_count, out_weight):
    rows, width = queries.shape
    devices = lax.axis_size("blk")
    plan = Plan(width // HD, devices)
    blocks = rows // BS
    table = jnp.concatenate([block_list, block_count[:, None]], axis=1)
    table = jnp.pad(table, ((0, META - blocks), (0, HD - KB - 1)))
    return project(attention(plan, queries, keys, values, table), out_weight)


def solution(mesh):
    placed = (
        P(("dp", "blk"), "head"),
        P(("dp", "blk"), "head"),
        P(("dp", "blk"), "head"),
        P(("dp", "blk"), None),
        P(("dp", "blk")),
        P("head", None),
    )
    return jax.shard_map(
        on_device,
        mesh=mesh,
        in_specs=placed,
        out_specs=P(("dp", "blk", "head"), None),
        check_vma=False,
    )
```
